128 devices in a mesh: row: 8 (over z, core), col: 16 (over x, y).
Axes of the slice: x: 4, y: 4, z: 4, core: 2. Of those that a mesh axis runs over, the one named last changes fastest.
Arguments:
- features: bfloat16 [12, 8, 256, 256], P(None, 'row', 'col'), may hold values from -6 to 6
Outputs:
- schur: float32 [12, 8, 256, 6, 16, 256], P(None, 'row', None, None, 'col')
- panels: float32 [12, 8, 256, 512], P(None, 'row')
The draws below stay inside these ranges and needn't reach their ends.
All inputs are finite; a program needn't handle non-finite values.
Results may differ from the reference program's by a relative error of at most 0.0033.
Values may be sent and summed in bfloat16 or wider, within the bound.
No kernel may reach another device: no remote copies, remote signals or barrier semaphores. Data moves between devices by JAX's collectives and lax.ppermute only.
A program may use at most 128 MiB of HBM per device.

```python
import jax
import jax.numpy as jnp
from jax import lax

TILE = 256
FEAT = 256
TR_DEV = 12
ORDER = 24576
TC_DEV = 6
N_ROW = 8
N_COL = 16


def block_levels(own_key, shape, cuts, least, largest):
    gain = 1.0
    for axis_at, parts in cuts:
        steps = jax.random.uniform(jax.random.fold_in(jax.random.fold_in(own_key, 6), axis_at), (parts,), jnp.float32, least / len(cuts), largest / len(cuts))
        gain = gain * jnp.repeat(jnp.exp(steps), shape[axis_at] // parts).reshape((-1,) + (1,) * (len(shape) - 1 - axis_at))
    return gain


def centred(rng, dims, deviation, reach, cuts=(), kind=jnp.bfloat16):
    level = block_levels(rng, dims, cuts, -0.22, 0.18) if cuts else 1.0
    entries = jax.random.normal(rng, dims, jnp.float32) * deviation * level
    return jnp.minimum(jnp.maximum(entries, -reach), reach).astype(kind)


def setup_inputs(seed: int = 0) -> dict:
    seeds = jax.random.split(jax.random.key(seed), 2)
    features = centred(seeds[0], (TR_DEV, N_ROW, TILE, FEAT), 1.0, 6.0, ((1, 8), (2, 16)))
    return dict(features=features)


kernel_gain = 2.0
epsilon = 1e-06

def kernel_block(row_feats, col_feats, row_start, col_start):
    products = jnp.dot(row_feats.astype(jnp.float32), col_feats.T.astype(jnp.float32), preferred_element_type=jnp.float32)
    values = jnp.exp(kernel_gain * (products - 1.0))
    row_index = row_start + jnp.arange(row_feats.shape[0], dtype=jnp.int32)[:, None]
    col_index = col_start + jnp.arange(col_feats.shape[0], dtype=jnp.int32)[None, :]
    return values + (row_index == col_index).astype(values.dtype)

def panel_factor(column, panel_index):
    start = panel_index * TILE
    factor = jnp.linalg.cholesky(column[start:start + TILE])
    solved = lax.linalg.triangular_solve(factor, column, left_side=False, lower=True, transpose_a=True)
    pieces = solved.reshape(ORDER // TILE, TILE, TILE)
    marker = jnp.arange(ORDER // TILE, dtype=jnp.int32)[:, None, None]
    pieces = jnp.where(marker == panel_index, factor[None], jnp.where(marker < panel_index, jnp.zeros_like(pieces), pieces))
    return pieces.reshape(ORDER, TILE)

def reference(features):
    floated = features.reshape(ORDER, FEAT).astype(jnp.float32)
    unit_rows = (floated * lax.rsqrt(lax.optimization_barrier(jnp.sum(floated * floated, axis=-1, keepdims=True)) + epsilon)).astype(jnp.bfloat16)
    front = kernel_block(unit_rows, unit_rows[:2 * TILE], jnp.int32(0), jnp.int32(0))
    first = panel_factor(front[:, :TILE], 0)
    col_next = front[:, TILE:] - jnp.dot(first, first[TILE:2 * TILE].T, precision=lax.Precision.HIGHEST)
    second = panel_factor(col_next, 1)
    both = jnp.concatenate([first, second], axis=1)

    def one_block(block_index):
        start = (block_index * TILE).astype(jnp.int32)
        row_feats = lax.dynamic_slice_in_dim(unit_rows, start, TILE, 0)
        block_kernel = kernel_block(row_feats, unit_rows, start, jnp.int32(0))
        block_panel = lax.dynamic_slice_in_dim(both, start, TILE, 0)
        return block_kernel - jnp.dot(block_panel, both.T, precision=lax.Precision.HIGHEST)
    schur = lax.map(one_block, jnp.arange(ORDER // TILE, dtype=jnp.int32)).reshape(ORDER, ORDER)
    return (schur.reshape(TR_DEV, N_ROW, TILE, TC_DEV, N_COL, TILE), both.reshape(TR_DEV, N_ROW, TILE, 2 * TILE))
```

```python
import functools

import jax
import jax.numpy as jnp
from jax import lax
from jax.experimental import pallas as pl
from jax.experimental.pallas import tpu as pltpu
from jax.sharding import PartitionSpec as P

T = 256
BF = jnp.bfloat16
F32 = jnp.float32

def dot_nt(a, b):
    return lax.dot_general(a, b, (((1,), (1,)), ((), ())), preferred_element_type=F32)

def split(x):
    hi = x.astype(BF)
    return hi, (x - hi.astype(F32)).astype(BF)

def kern(u, v):
    return jnp.exp(2.0 * dot_nt(u, v) - 2.0)

def eye_mask(n):
    return lax.broadcasted_iota(jnp.int32, (n, n), 0) == lax.broadcasted_iota(jnp.int32, (n, n), 1)

def panel_rows(k, xh, xl):
    kh, kl = split(k)
    out = []
    for b in range(2):
        n = (b + 1) * T
        rs = slice(b * T, (b + 1) * T)
        a = dot_nt(kh[:, :n], xh[rs, :n]) + dot_nt(kl[:, :n], xh[rs, :n]) + dot_nt(kh[:, :n], xl[rs, :n])
        out.append(a)
    return out

def schur_kernel(pos, urow, ucol, u0, xh, xl, schur, pan, pch, pcl, *, tiles_r, mode="strided"):
    step = pl.program_id(0)
    r, c = pos[0], pos[1]
    @pl.when(step == 0)
    def _():
        for j in range(6):
            k = kern(ucol[:, j].reshape(T, T), u0[...])
            if j == 0:
                tile = c
                rows = lax.broadcasted_iota(jnp.int32, (T, 2 * T), 0) + tile * T
                cols = lax.broadcasted_iota(jnp.int32, (T, 2 * T), 1)
                k = k + (rows == cols).astype(F32)
            p0, p1 = panel_rows(k, xh, xl)
            h0, l0 = split(p0)
            h1, l1 = split(p1)
            pch[j, :, 0:T] = h0
            pch[j, :, T:] = h1
            pcl[j, :, 0:T] = l0
            pcl[j, :, T:] = l1
    for t in range(tiles_r):
        a = step * tiles_r + t
        tile = a * 8 + r
        u = urow[:, t].reshape(T, T)
        k = kern(u, u0[...])
        rows = lax.broadcasted_iota(jnp.int32, (T, 2 * T), 0) + tile * T
        cols = lax.broadcasted_iota(jnp.int32, (T, 2 * T), 1)
        k = k + (rows == cols).astype(F32)
        p0, p1 = panel_rows(k, xh, xl)
        p = jnp.concatenate([p0, p1], axis=1)
        p = jnp.where(rows >= cols, p, 0.0)
        pan[t] = p
        ph, plo = split(p)
        for j in range(6):
            kk = kern(u, ucol[:, j].reshape(T, T))
            coef = jnp.where(tile == j * 16 + c, 1.0, 0.0).astype(F32)
            s = kk + jnp.where(eye_mask(T), coef, 0.0)
            s = s - (dot_nt(ph, pch[j]) + dot_nt(plo, pch[j]) + dot_nt(ph, pcl[j]))
            if mode == "strided":
                for h in range(2):
                    schur[pl.ds(t * T * 12 + j * 2 + h, T, stride=12), :] = s[:, h * 128:(h + 1) * 128]
            else:
                schur[pl.ds(t * T * 12 + j * 512, T), :] = s[:, :128]
                schur[pl.ds(t * T * 12 + j * 512 + T, T), :] = s[:, 128:]

def schur_call(pos, urow, ucol, u0, xh, xl, tiles_r=1, mode="strided"):
    full = lambda s: pl.BlockSpec(s, lambda i, _: (0,) * len(s))
    return pl.pallas_call(
        functools.partial(schur_kernel, tiles_r=tiles_r, mode=mode),
        grid_spec=pltpu.PrefetchScalarGridSpec(
            num_scalar_prefetch=1,
            grid=(12 // tiles_r,),
            in_specs=[
                pl.BlockSpec((16, tiles_r, 16, T), lambda i, _: (0, i, 0, 0)),
                full((16, 6, 16, T)), full((2 * T, T)), full((2 * T, 2 * T)), full((2 * T, 2 * T)),
            ],
            out_specs=[
                pl.BlockSpec((tiles_r * T * 12, 128), lambda i, _: (i, 0)),
                pl.BlockSpec((tiles_r, T, 2 * T), lambda i, _: (i, 0, 0)),
            ],
            scratch_shapes=[pltpu.VMEM((6, T, 2 * T), BF), pltpu.VMEM((6, T, 2 * T), BF)],
        ),
        out_shape=[
            jax.ShapeDtypeStruct((12 * T * 12, 128), F32),
            jax.ShapeDtypeStruct((12, T, 2 * T), F32),
        ],
        compiler_params=pltpu.CompilerParams(vmem_limit_bytes=56 * 2**20, dimension_semantics=("arbitrary",)),
        name="schur",
    )(pos, urow, ucol, u0, xh, xl)


N = 512
B = 128
G = 8

def dot3(a, b, dims):
    ah, al = split(a)
    bh, bl = split(b)
    d = lambda x, y: lax.dot_general(x, y, (dims, ((), ())), preferred_element_type=F32)
    return d(ah, bh) + d(al, bh) + d(ah, bl)

def factor_block(a, b=None, width=B):
    eye = (lax.broadcasted_iota(jnp.int32, (B, B), 0) == lax.broadcasted_iota(jnp.int32, (B, B), 1)).astype(F32)
    groups_a = [a[G * g:G * g + G] for g in range(B // G)]
    groups_b = [eye[G * g:G * g + G] for g in range(B // G)]
    sub = lax.broadcasted_iota(jnp.int32, (G, B), 0)
    out = []
    n_g = B // G
    for g in range(n_g):
        cols = [[jnp.broadcast_to(groups_a[i][:, G * g + k:G * g + k + 1], (G, B)) for i in range(g, n_g)] for k in range(G)]
        rows_a = [groups_a[g][k:k + 1] for k in range(G)]
        rows_b = [groups_b[g][k:k + 1] for k in range(G)]
        facs = []
        scaled = []
        for k in range(G):
            d = cols[k][0][k:k + 1]
            rs = lax.rsqrt(d)
            r = rs * rs
            fac = [x * r for x in cols[k]]
            facs.append(fac)
            for m in range(k + 1, G):
                piv = cols[m][0][k:k + 1]
                cols[m] = [x - f * piv for x, f in zip(cols[m], fac)]
                f_m = fac[0][m:m + 1]
                rows_a[m] = rows_a[m] - f_m * rows_a[k]
                rows_b[m] = rows_b[m] - f_m * rows_b[k]
            scaled.append(rows_b[k] * rs)
        out.append(jnp.concatenate(scaled, axis=0))
        for i in range(g + 1, n_g):
            ga, gb = groups_a[i], groups_b[i]
            for k in range(G):
                ga = ga - facs[k][i - g] * rows_a[k]
                gb = gb - facs[k][i - g] * rows_b[k]
            groups_a[i], groups_b[i] = ga, gb
    return jnp.concatenate(out, axis=0)

def chol_kernel(u0, xh, xl, m):
    u = u0[...]
    row = lax.broadcasted_iota(jnp.int32, (N, N), 0)
    col = lax.broadcasted_iota(jnp.int32, (N, N), 1)
    eye = (row == col).astype(F32)
    m[:, :N] = kern(u, u) + eye
    m[:, N:] = eye
    for kb in range(N // B):
        rs = slice(kb * B, (kb + 1) * B)
        x = factor_block(m[rs, rs])
        hi_c = N + kb * B
        m[rs, kb * B:hi_c + B] = dot3(x, m[rs, kb * B:hi_c + B], ((1,), (0,)))
        if kb < N // B - 1:
            w = m[rs, (kb + 1) * B:hi_c + B]
            m[(kb + 1) * B:, (kb + 1) * B:hi_c + B] -= dot3(m[rs, (kb + 1) * B:N], w, ((0,), (0,)))
    x = jnp.where(row >= col, m[:, N:], 0.0)
    h, l = split(x)
    xh[...] = h
    xl[...] = l

def chol_call(u0):
    return pl.pallas_call(
        chol_kernel,
        out_shape=[jax.ShapeDtypeStruct((N, N), BF)] * 2,
        in_specs=[pl.BlockSpec(memory_space=pltpu.VMEM)],
        out_specs=[pl.BlockSpec(memory_space=pltpu.VMEM)] * 2,
        scratch_shapes=[pltpu.VMEM((N, 2 * N), F32)],
        compiler_params=pltpu.CompilerParams(vmem_limit_bytes=40 * 2**20),
        name="factor",
    )(u0)


epsilon = 1e-06


def swap_row(value, flip_z, flip_core):
    pairs = [(r, (((r >> 1) ^ flip_z) << 1) | ((r & 1) ^ flip_core)) for r in range(8)]
    return lax.ppermute(value, "row", pairs)


def swap_col(value, flip_x, flip_y):
    pairs = [(c, (((c >> 2) ^ flip_x) << 2) | ((c & 3) ^ flip_y)) for c in range(16)]
    return lax.ppermute(value, "col", pairs)


def ordered(mine, other, second, axis=0):
    first = jnp.where(second, other, mine)
    last = jnp.where(second, mine, other)
    return jnp.concatenate([first, last], axis=axis)


def per_device(features):
    r = lax.axis_index("row")
    c = lax.axis_index("col")
    z, core = r // 2, r % 2
    x, y = c // 4, c % 4
    floated = features[:, 0].astype(F32)
    unit = (
        floated * lax.rsqrt(jnp.sum(floated * floated, axis=-1, keepdims=True) + epsilon)
    ).astype(BF)

    first = unit[0][None]
    first = ordered(first, swap_row(first, 0, 1), core == 1)
    first = jnp.where(z % 2 == 1, swap_row(first, 1, 0), first)
    first = jnp.where(z >= 2, swap_row(first, 3, 0), first)
    first = first[None]
    first = ordered(first, swap_col(first, 0, 1), y % 2 == 1)
    first = ordered(first, swap_col(first, 0, 3), y >= 2)
    first = ordered(first, swap_col(first, 1, 0), x % 2 == 1)
    first = ordered(first, swap_col(first, 3, 0), x >= 2)
    front = first.transpose(1, 0, 2, 3).reshape(2 * T, T)

    rows = unit[None]
    rows = ordered(rows, swap_col(rows, 1, 0), x % 2 == 1, 0)
    rows = ordered(rows, swap_col(rows, 3, 0), x >= 2, 0)
    rows = rows[:, None]
    rows = ordered(rows, swap_col(rows, 0, 1), y % 2 == 1, 1)
    rows = ordered(rows, swap_col(rows, 0, 3), y >= 2, 1)
    rows = rows.reshape(16, 12, 16, T)

    half = c // 8
    pieces = unit.reshape(6, 2, 16, T)
    even = c % 2 == 0
    piece_a = jnp.where(even, pieces[:, 0], pieces[:, 1])
    piece_b = jnp.where(even, pieces[:, 1], pieces[:, 0])
    route_a = [(q * 16 + s, (s // 2) * 16 + (s % 2) * 8 + q) for q in range(8) for s in range(16)]
    route_b = [(q * 16 + s, (s // 2) * 16 + (1 - s % 2) * 8 + q) for q in range(8) for s in range(16)]
    got_a = lax.ppermute(piece_a, ("row", "col"), route_a)[None]
    got_b = lax.ppermute(piece_b, ("row", "col"), route_b)[None]
    cols = ordered(got_a, got_b, half == 1)[None]
    cols = ordered(cols, swap_row(cols, 1, 0), z % 2 == 1)
    cols = ordered(cols, swap_row(cols, 3, 0), z >= 2)
    cols = cols[:, None]
    cols = ordered(cols, swap_row(cols, 0, 1), core == 1, 1)
    cols = cols.reshape(16, 6, 16, T)

    xh, xl = chol_call(front)
    pos = jnp.stack([r, c]).astype(jnp.int32)
    schur, panels = schur_call(pos, rows, cols, front, xh, xl)
    return schur.reshape(12, 1, T, 6, 1, T), panels[:, None]


def solution(mesh):
    return jax.shard_map(
        per_device,
        mesh=mesh,
        in_specs=(P(None, "row", "col", None),),
        out_specs=(P(None, "row", None, None, "col", None), P(None, "row", None, None)),
        check_vma=False,
    )
```

```python
import functools

import jax
import jax.numpy as jnp
from jax import lax
from jax.experimental import pallas as pl
from jax.experimental.pallas import tpu as pltpu
from jax.sharding import PartitionSpec as P

T = 256
N = 2 * T
B = 128
G = 8
BF = jnp.bfloat16
F32 = jnp.float32
SCALE = 2.0 * 1.4426950408889634
epsilon = 1e-06


def dot_nt(a, b):
    return lax.dot_general(a, b, (((1,), (1,)), ((), ())), preferred_element_type=F32)


def split(x):
    hi = x.astype(BF)
    return hi, (x - hi.astype(F32)).astype(BF)


def kern(u, v):
    return jnp.exp2(SCALE * dot_nt(u, v) - SCALE)


def normal(raw):
    f = raw.astype(F32)
    return (f * lax.rsqrt(jnp.sum(f * f, axis=-1, keepdims=True) + epsilon)).astype(BF)


def dot3(a, b, dims):
    ah, al = split(a)
    bh, bl = split(b)
    d = lambda x, y: lax.dot_general(x, y, (dims, ((), ())), preferred_element_type=F32)
    return d(ah, bh) + d(al, bh) + d(ah, bl)


def factor_block(a):
    eye = (lax.broadcasted_iota(jnp.int32, (B, B), 0) == lax.broadcasted_iota(jnp.int32, (B, B), 1)).astype(F32)
    n_g = B // G
    groups_a = [a[G * g : G * g + G] for g in range(n_g)]
    groups_b = [eye[G * g : G * g + G] for g in range(n_g)]
    out = []
    for g in range(n_g):
        cols = [
            [jnp.broadcast_to(groups_a[i][:, G * g + k : G * g + k + 1], (G, B)) for i in range(g, n_g)]
            for k in range(G)
        ]
        rows_a = [groups_a[g][k : k + 1] for k in range(G)]
        rows_b = [groups_b[g][k : k + 1] for k in range(G)]
        facs = []
        for k in range(G):
            scale = lax.rsqrt(cols[k][0][k : k + 1])
            fac = [x * scale for x in cols[k]]
            facs.append(fac)
            rows_a[k] = rows_a[k] * scale
            rows_b[k] = rows_b[k] * scale
            for m in range(k + 1, G):
                piv = fac[0][m : m + 1]
                cols[m] = [x - f * piv for x, f in zip(cols[m], fac)]
                rows_a[m] = rows_a[m] - piv * rows_a[k]
                rows_b[m] = rows_b[m] - piv * rows_b[k]
        out.append(jnp.concatenate(rows_b, axis=0))
        for i in range(g + 1, n_g):
            ga, gb = groups_a[i], groups_b[i]
            for k in range(G):
                ga = ga - facs[k][i - g] * rows_a[k]
                gb = gb - facs[k][i - g] * rows_b[k]
            groups_a[i], groups_b[i] = ga, gb
    return jnp.concatenate(out, axis=0)


def thrice(x, left):
    hi, lo = split(x)
    return jnp.concatenate([hi, lo, hi] if left else [hi, hi, lo], axis=1)


def picked(flag, second, mine, other):
    return jnp.where(flag, mine, other) if second else jnp.where(flag, other, mine)


def eliminate(top, k):
    w = dot3(top, k[:B, B:], ((1,), (0,)))
    return w, k[B:, B:] - dot3(w, w, ((0,), (0,)))


def joined(top, w, bottom):
    corner = dot3(bottom, dot3(w, top, ((0,), (0,))), ((1,), (0,)))
    return jnp.concatenate(
        [jnp.concatenate([top, jnp.zeros((B, B), F32)], axis=1), jnp.concatenate([-corner, bottom], axis=1)], axis=0
    )


def identity():
    return (lax.broadcasted_iota(jnp.int32, (T, T), 0) == lax.broadcasted_iota(jnp.int32, (T, T), 1)).astype(F32)


def factor_start(pos, mine, other, u0, top, w, rest):
    x = pos[1] // 4
    inner = jnp.logical_or(x == 1, x == 2)
    for t in range(2):
        for c in range(16):
            x, y = c // 4, c % 4
            block = picked(inner, int(x in (1, 2)), mine[x // 2, y, t], other[x // 2, y, t])
            u0[t * T + c * 16 : t * T + c * 16 + 16, :] = normal(block)
    u = u0[:T, :]
    k = kern(u, u) + identity()
    top[...] = factor_block(k[:B, :B])
    w[...], rest[...] = eliminate(top[...], k)


def factor_middle(u0, top, w, rest, x0, lx, d1):
    u = u0[...]
    k10 = kern(u[T:], u[:T])
    k11 = kern(u[T:], u[T:]) + identity()
    x = joined(top[...], w[...], factor_block(rest[...]))
    x0[...] = thrice(x, False)
    low = dot_nt(thrice(k10, True), x0[...])
    lx[...] = dot3(low, x, ((1,), (0,)))
    d1[...] = k11 - dot_nt(thrice(low, True), thrice(low, False))


def factor_next(d1, top, w, rest):
    d = d1[...]
    top[...] = factor_block(d[:B, :B])
    w[...], rest[...] = eliminate(top[...], d)


def factor_end(top, w, rest, lx, x1):
    x = joined(top[...], w[...], factor_block(rest[...]))
    x1[...] = thrice(jnp.concatenate([-dot3(x, lx[...], ((1,), (0,))), x], axis=1), False)


def factor_call(kernel, name, outs, *args):
    vmem = pl.BlockSpec(memory_space=pltpu.VMEM)
    place = lambda a: pl.BlockSpec(memory_space=pltpu.SMEM) if a.dtype == jnp.int32 else vmem
    return pl.pallas_call(
        kernel,
        out_shape=[jax.ShapeDtypeStruct(*o) for o in outs],
        in_specs=[place(a) for a in args],
        out_specs=[vmem] * len(outs),
        compiler_params=pltpu.CompilerParams(vmem_limit_bytes=16 * 2**20),
        cost_estimate=pl.CostEstimate(flops=4 * 10**9, bytes_accessed=10**6, transcendentals=T * N),
        name=name,
    )(*args)


def panel_rows(k, xs):
    kh, kl = split(k)
    out = []
    for b in range(2):
        n = (b + 1) * T
        out.append(dot_nt(jnp.concatenate([kh[:, :n], kl[:, :n], kh[:, :n]], axis=1), xs[b][...]))
    return out


def schur_kernel(pos, row_mine, row_other, col_mine, col_other, u0, x0, x1, schur, pan, pc, uc, *, tiles):
    step = pl.program_id(0)
    r, c = pos[0], pos[1]
    height = tiles * T

    @pl.when(step == 0)
    def _():
        core = r % 2 == 1
        for j in range(6):
            for s in range(16):
                z, e = s // 4, s % 2
                low, high = col_mine[z, e, j], col_other[z, e, j]
                block = picked(core, (s // 2) % 2, low, high)
                uc[j, s * 16 : s * 16 + 16, :] = normal(block)
            k = kern(uc[j], u0[...])
            if j == 0:
                rows = lax.broadcasted_iota(jnp.int32, (T, N), 0) + c * T
                k = k + (rows == lax.broadcasted_iota(jnp.int32, (T, N), 1)).astype(F32)
            (h0, l0), (h1, l1) = [split(p) for p in panel_rows(k, (x0, x1))]
            pc[j] = jnp.concatenate([h0, h1, h0, h1, l0, l1], axis=1)

    x_hi = c // 4 >= 2
    blocks = []
    for t in range(tiles):
        for s in range(16):
            x, y = s // 4, s % 4
            low, high = row_mine[x % 2, y, t], row_other[x % 2, y, t]
            blocks.append(picked(x_hi, x // 2, low, high))
    u = normal(jnp.concatenate(blocks, axis=0))
    k = kern(u, u0[...])
    rows = lax.broadcasted_iota(jnp.int32, (height, N), 0)
    cols = lax.broadcasted_iota(jnp.int32, (height, N), 1)
    shift = jnp.where(jnp.logical_and(step == 0, r < 2), r * T, N)
    rows = rows + jnp.where(rows < T, shift, N)
    k = k + (rows == cols).astype(F32)
    p = jnp.concatenate(panel_rows(k, (x0, x1)), axis=1)
    p = jnp.where(rows >= cols, p, 0.0)
    for t in range(tiles):
        pan[t] = p[t * T : (t + 1) * T]
    hi, lo = split(p)
    left = jnp.concatenate([hi, lo, hi], axis=1)
    for j in range(6):
        s = kern(u, uc[j]) - dot_nt(left, pc[j])
        for t in range(tiles):
            for h in range(2):
                schur[pl.ds(t * T * 12 + j * 2 + h, T, stride=12), :] = s[t * T : (t + 1) * T, h * 128 : h * 128 + 128]
    for t in range(tiles):
        a = step * tiles + t

        @pl.when(jnp.logical_and(r == c % 8, (a - c // 8) % 2 == 0))
        def _():
            j = (a - c // 8) // 2
            for h in range(2):
                where = pl.ds(t * T * 12 + j * 2 + h, T, stride=12)
                i = lax.broadcasted_iota(jnp.int32, (T, 128), 0)
                l = lax.broadcasted_iota(jnp.int32, (T, 128), 1) + h * 128
                schur[where, :] = schur[where, :] + (i == l).astype(F32)


def schur_call(pos, row_mine, row_other, col_mine, col_other, u0, x0, x1, tiles=2):
    full = lambda a: pl.BlockSpec(a.shape, lambda i, _: (0,) * a.ndim)
    rows = pl.BlockSpec((2, 4, tiles, 16, T), lambda i, _: (0, 0, i, 0, 0))
    return pl.pallas_call(
        functools.partial(schur_kernel, tiles=tiles),
        grid_spec=pltpu.PrefetchScalarGridSpec(
            num_scalar_prefetch=1,
            grid=(12 // tiles,),
            in_specs=[rows, rows] + [full(a) for a in (col_mine, col_other, u0, x0, x1)],
            out_specs=[
                pl.BlockSpec((tiles * T * 12, 128), lambda i, _: (i, 0)),
                pl.BlockSpec((tiles, T, N), lambda i, _: (i, 0, 0)),
            ],
            scratch_shapes=[pltpu.VMEM((6, T, 6 * T), BF), pltpu.VMEM((6, T, T), BF)],
        ),
        out_shape=[
            jax.ShapeDtypeStruct((12 * T * 12, 128), F32),
            jax.ShapeDtypeStruct((12, T, N), F32),
        ],
        compiler_params=pltpu.CompilerParams(vmem_limit_bytes=40 * 2**20, dimension_semantics=("arbitrary",)),
        cost_estimate=pl.CostEstimate(flops=24 * 10**9, bytes_accessed=30 * 10**6, transcendentals=7 * 10**6),
        name="schur",
    )(pos, row_mine, row_other, col_mine, col_other, u0, x0, x1)


def swap_row(value, flip_z, flip_core):
    pairs = [(r, (((r >> 1) ^ flip_z) << 1) | ((r & 1) ^ flip_core)) for r in range(8)]
    return lax.ppermute(value, "row", pairs)


def swap_col(value, flip_x, flip_y):
    pairs = [(c, (((c >> 2) ^ flip_x) << 2) | ((c & 3) ^ flip_y)) for c in range(16)]
    return lax.ppermute(value, "col", pairs)


def ordered(mine, other, second):
    return jnp.stack([jnp.where(second, other, mine), jnp.where(second, mine, other)])


def after(value, *earlier):
    return lax.optimization_barrier((value,) + earlier)[0]


def per_device(features):
    r = lax.axis_index("row")
    c = lax.axis_index("col")
    z, core = r // 2, r % 2
    x, y = c // 4, c % 4
    pos = jnp.stack([r, c]).astype(jnp.int32)
    own = features[:, 0]

    together = lambda *values: lax.optimization_barrier(values)

    first_a = own[0]
    first_b = swap_row(first_a, 0, 1)
    rows_b = swap_col(own, 0, 1)
    first = ordered(first_a, first_b, core == 1)

    got = swap_row(first, 1, 0)
    first, rows_b = together(jnp.where(z % 2 == 1, got, first), rows_b)

    got = swap_row(first, 3, 0)
    rows = ordered(own, rows_b, y % 2 == 1)
    pair = rows.reshape(2, 6, 2, 16, T)
    rows_b = swap_col(rows, 0, 3)
    first, rows_b = together(jnp.where(z >= 2, got, first), rows_b)

    first_b = swap_col(first, 0, 1)
    rows = ordered(rows, rows_b, y >= 2).reshape(4, 12, 16, T)
    rows_b = swap_col(rows, 1, 0)
    first = ordered(first, first_b, y % 2 == 1)

    first_b = swap_col(first, 0, 3)
    first = ordered(first, first_b, y >= 2).reshape(4, 2, 16, T)

    first_b = swap_col(first, 3, 0)
    first, rows_b = together(ordered(first, first_b, x >= 2), rows_b)

    first_b = swap_col(first, 1, 0)
    rows = ordered(rows, rows_b, x % 2 == 1)
    rows_b = swap_col(rows, 3, 0)
    pair = after(jnp.where(c % 2 == 1, pair[:, :, 1], pair[:, :, 0]), first)
    route = [(q * 16 + s, (s // 2) * 16 + (s % 2) * 8 + q) for q in range(8) for s in range(16)]
    cols = lax.ppermute(pair, ("row", "col"), route)

    small = [((B, B), F32)] * 3
    u0, *state = factor_call(factor_start, "factor_start", [((N, T), BF)] + small, pos, first, first_b)
    u0, cols = together(u0, cols)
    cols_b = swap_row(cols, 1, 0)
    x0, lx, d1 = factor_call(
        factor_middle, "factor_middle", [((T, 3 * T), BF), ((T, T), F32), ((T, T), F32)], u0, *state
    )
    d1, cols_b = together(d1, cols_b)
    cols = ordered(cols, cols_b, z % 2 == 1)
    cols_b = swap_row(cols, 3, 0)
    state = factor_call(factor_next, "factor_next", small, d1)
    *state, cols_b = together(*state, cols_b)
    cols = ordered(cols, cols_b, z >= 2).reshape(4, 2, 6, 16, T)
    cols_b = swap_row(cols, 0, 1)
    (x1,) = factor_call(factor_end, "factor_end", [((T, 6 * T), BF)], *state, lx)

    schur, panels = schur_call(pos, rows, rows_b, cols, cols_b, u0, x0, x1)
    return schur.reshape(12, 1, T, 6, 1, T), panels[:, None]


def solution(mesh):
    return jax.shard_map(
        per_device,
        mesh=mesh,
        in_specs=(P(None, "row", "col", None),),
        out_specs=(P(None, "row", None, None, "col", None), P(None, "row", None, None)),
        check_vma=False,
    )
```

```python
import functools

import jax
import jax.numpy as jnp
from jax import lax
from jax.experimental import pallas as pl
from jax.experimental.pallas import tpu as pltpu
from jax.sharding import PartitionSpec as P

T = 256
N = 2 * T
B = 128
G = 8
BF = jnp.bfloat16
F32 = jnp.float32
SCALE = 2.0 * 1.4426950408889634
epsilon = 1e-06


def dot_nt(a, b):
    return lax.dot_general(a, b, (((1,), (1,)), ((), ())), preferred_element_type=F32)


def split(x):
    hi = x.astype(BF)
    return hi, (x - hi.astype(F32)).astype(BF)


def kern(u, v):
    return jnp.exp2(SCALE * dot_nt(u, v) - SCALE)


def normal(raw):
    f = raw.astype(F32)
    return (f * lax.rsqrt(jnp.sum(f * f, axis=-1, keepdims=True) + epsilon)).astype(BF)


def dot3(a, b, dims):
    ah, al = split(a)
    bh, bl = split(b)
    d = lambda x, y: lax.dot_general(x, y, (dims, ((), ())), preferred_element_type=F32)
    return d(ah, bh) + d(al, bh) + d(ah, bl)


def factor_block(a):
    eye = (lax.broadcasted_iota(jnp.int32, (B, B), 0) == lax.broadcasted_iota(jnp.int32, (B, B), 1)).astype(F32)
    n_g = B // G
    groups_a = [a[G * g : G * g + G] for g in range(n_g)]
    groups_b = [eye[G * g : G * g + G] for g in range(n_g)]
    out = []
    for g in range(n_g):
        cols = [
            [jnp.broadcast_to(groups_a[i][:, G * g + k : G * g + k + 1], (G, B)) for i in range(g, n_g)]
            for k in range(G)
        ]
        rows_a = [groups_a[g][k : k + 1] for k in range(G)]
        rows_b = [groups_b[g][k : k + 1] for k in range(G)]
        facs = []
        for k in range(G):
            scale = lax.rsqrt(cols[k][0][k : k + 1])
            fac = [x * scale for x in cols[k]]
            facs.append(fac)
            rows_a[k] = rows_a[k] * scale
            rows_b[k] = rows_b[k] * scale
            for m in range(k + 1, G):
                piv = fac[0][m : m + 1]
                cols[m] = [x - f * piv for x, f in zip(cols[m], fac)]
                rows_a[m] = rows_a[m] - piv * rows_a[k]
                rows_b[m] = rows_b[m] - piv * rows_b[k]
        out.append(jnp.concatenate(rows_b, axis=0))
        for i in range(g + 1, n_g):
            ga, gb = groups_a[i], groups_b[i]
            for k in range(G):
                ga = ga - facs[k][i - g] * rows_a[k]
                gb = gb - facs[k][i - g] * rows_b[k]
            groups_a[i], groups_b[i] = ga, gb
    return jnp.concatenate(out, axis=0)


def thrice(x, left):
    hi, lo = split(x)
    return jnp.concatenate([hi, lo, hi] if left else [hi, hi, lo], axis=1)


def picked(flag, second, mine, other):
    return jnp.where(flag, mine, other) if second else jnp.where(flag, other, mine)


def eliminate(top, k):
    w = dot3(top, k[:B, B:], ((1,), (0,)))
    return w, k[B:, B:] - dot3(w, w, ((0,), (0,)))


def joined(top, w, bottom):
    corner = dot3(bottom, dot3(w, top, ((0,), (0,))), ((1,), (0,)))
    return jnp.concatenate(
        [jnp.concatenate([top, jnp.zeros((B, B), F32)], axis=1), jnp.concatenate([-corner, bottom], axis=1)], axis=0
    )


def identity():
    return (lax.broadcasted_iota(jnp.int32, (T, T), 0) == lax.broadcasted_iota(jnp.int32, (T, T), 1)).astype(F32)


def factor_start(pos, mine, other, u0, top, w, rest):
    x = pos[1] // 4
    inner = jnp.logical_or(x == 1, x == 2)
    for t in range(2):
        for c in range(16):
            x, y = c // 4, c % 4
            block = picked(inner, int(x in (1, 2)), mine[x // 2, y, t], other[x // 2, y, t])
            u0[t * T + c * 16 : t * T + c * 16 + 16, :] = normal(block)
    u = u0[:T, :]
    k = kern(u, u) + identity()
    top[...] = factor_block(k[:B, :B])
    w[...], rest[...] = eliminate(top[...], k)


def factor_middle(u0, top, w, rest, x0, lx, d1):
    u = u0[...]
    k10 = kern(u[T:], u[:T])
    k11 = kern(u[T:], u[T:]) + identity()
    x = joined(top[...], w[...], factor_block(rest[...]))
    x0[...] = thrice(x, False)
    low = dot_nt(thrice(k10, True), x0[...])
    lx[...] = dot3(low, x, ((1,), (0,)))
    d1[...] = k11 - dot_nt(thrice(low, True), thrice(low, False))


def factor_next(d1, top, w, rest):
    d = d1[...]
    top[...] = factor_block(d[:B, :B])
    w[...], rest[...] = eliminate(top[...], d)


def factor_end(top, w, rest, lx, x1):
    x = joined(top[...], w[...], factor_block(rest[...]))
    x1[...] = thrice(jnp.concatenate([-dot3(x, lx[...], ((1,), (0,))), x], axis=1), False)


def factor_call(kernel, name, outs, *args):
    vmem = pl.BlockSpec(memory_space=pltpu.VMEM)
    place = lambda a: pl.BlockSpec(memory_space=pltpu.SMEM) if a.dtype == jnp.int32 else vmem
    return pl.pallas_call(
        kernel,
        out_shape=[jax.ShapeDtypeStruct(*o) for o in outs],
        in_specs=[place(a) for a in args],
        out_specs=[vmem] * len(outs),
        compiler_params=pltpu.CompilerParams(vmem_limit_bytes=16 * 2**20),
        cost_estimate=pl.CostEstimate(flops=4 * 10**9, bytes_accessed=10**6, transcendentals=T * N),
        name=name,
    )(*args)


def panel_rows(k, xs):
    kh, kl = split(k)
    out = []
    for b in range(2):
        n = (b + 1) * T
        out.append(dot_nt(jnp.concatenate([kh[:, :n], kl[:, :n], kh[:, :n]], axis=1), xs[b][...]))
    return out


def schur_kernel(pos, row_mine, row_other, col_mine, col_other, u0, x0, x1, schur, pan, pc, uc, *, tiles):
    step = pl.program_id(0)
    r, c = pos[0], pos[1]
    height = tiles * T

    @pl.when(step == 0)
    def _():
        for j in range(6):
            for s in range(16):
                host = pos[2 + c * 8 + s // 2]
                z, e = host // 2, s % 2
                block = jnp.where(host % 2 == r % 2, col_mine[z, e, j], col_other[z, e, j])
                uc[j, s * 16 : s * 16 + 16, :] = normal(block)
            k = kern(uc[j], u0[...])
            if j == 0:
                rows = lax.broadcasted_iota(jnp.int32, (T, N), 0) + c * T
                k = k + (rows == lax.broadcasted_iota(jnp.int32, (T, N), 1)).astype(F32)
            (h0, l0), (h1, l1) = [split(p) for p in panel_rows(k, (x0, x1))]
            pc[j] = jnp.concatenate([h0, h1, h0, h1, l0, l1], axis=1)

    x_hi = c // 4 >= 2
    blocks = []
    for t in range(tiles):
        for s in range(16):
            x, y = s // 4, s % 4
            low, high = row_mine[x % 2, y, t], row_other[x % 2, y, t]
            blocks.append(picked(x_hi, x // 2, low, high))
    u = normal(jnp.concatenate(blocks, axis=0))
    k = kern(u, u0[...])
    rows = lax.broadcasted_iota(jnp.int32, (height, N), 0)
    cols = lax.broadcasted_iota(jnp.int32, (height, N), 1)
    shift = jnp.where(jnp.logical_and(step == 0, r < 2), r * T, N)
    rows = rows + jnp.where(rows < T, shift, N)
    k = k + (rows == cols).astype(F32)
    p = jnp.concatenate(panel_rows(k, (x0, x1)), axis=1)
    p = jnp.where(rows >= cols, p, 0.0)
    for t in range(tiles):
        pan[t] = p[t * T : (t + 1) * T]
    hi, lo = split(p)
    left = jnp.concatenate([hi, lo, hi], axis=1)
    for j in range(6):
        s = kern(u, uc[j]) - dot_nt(left, pc[j])
        for t in range(tiles):
            for h in range(2):
                schur[pl.ds(t * T * 12 + j * 2 + h, T, stride=12), :] = s[t * T : (t + 1) * T, h * 128 : h * 128 + 128]
    for t in range(tiles):
        a = step * tiles + t

        @pl.when(jnp.logical_and(r == c % 8, (a - c // 8) % 2 == 0))
        def _():
            j = (a - c // 8) // 2
            for h in range(2):
                where = pl.ds(t * T * 12 + j * 2 + h, T, stride=12)
                i = lax.broadcasted_iota(jnp.int32, (T, 128), 0)
                l = lax.broadcasted_iota(jnp.int32, (T, 128), 1) + h * 128
                schur[where, :] = schur[where, :] + (i == l).astype(F32)


def schur_call(pos, row_mine, row_other, col_mine, col_other, u0, x0, x1, tiles=2):
    full = lambda a: pl.BlockSpec(a.shape, lambda i, _: (0,) * a.ndim)
    rows = pl.BlockSpec((2, 4, tiles, 16, T), lambda i, _: (0, 0, i, 0, 0))
    return pl.pallas_call(
        functools.partial(schur_kernel, tiles=tiles),
        grid_spec=pltpu.PrefetchScalarGridSpec(
            num_scalar_prefetch=1,
            grid=(12 // tiles,),
            in_specs=[rows, rows] + [full(a) for a in (col_mine, col_other, u0, x0, x1)],
            out_specs=[
                pl.BlockSpec((tiles * T * 12, 128), lambda i, _: (i, 0)),
                pl.BlockSpec((tiles, T, N), lambda i, _: (i, 0, 0)),
            ],
            scratch_shapes=[pltpu.VMEM((6, T, 6 * T), BF), pltpu.VMEM((6, T, T), BF)],
        ),
        out_shape=[
            jax.ShapeDtypeStruct((12 * T * 12, 128), F32),
            jax.ShapeDtypeStruct((12, T, N), F32),
        ],
        compiler_params=pltpu.CompilerParams(vmem_limit_bytes=40 * 2**20, dimension_semantics=("arbitrary",)),
        cost_estimate=pl.CostEstimate(flops=24 * 10**9, bytes_accessed=30 * 10**6, transcendentals=7 * 10**6),
        name="schur",
    )(pos, row_mine, row_other, col_mine, col_other, u0, x0, x1)


def hops(a, b):
    return min((a - b) % 4, (b - a) % 4)


def host_rows(column):
    row, odd = column % 8, column // 8
    far = lambda p: hops(p // 2, column // 4) + hops(p % 2 * 2 + odd, column % 4)
    pairs = sorted(range(8), key=lambda p: (-far(p), p))
    rows = sorted(range(8), key=lambda r: (hops(r // 2, row // 2), r))
    return [rows[pairs.index(p)] for p in range(8)]


HOSTS = [host_rows(column) for column in range(16)]


def swap_row(value, flip_z, flip_core):
    pairs = [(r, (((r >> 1) ^ flip_z) << 1) | ((r & 1) ^ flip_core)) for r in range(8)]
    return lax.ppermute(value, "row", pairs)


def swap_col(value, flip_x, flip_y):
    pairs = [(c, (((c >> 2) ^ flip_x) << 2) | ((c & 3) ^ flip_y)) for c in range(16)]
    return lax.ppermute(value, "col", pairs)


def ordered(mine, other, second):
    return jnp.stack([jnp.where(second, other, mine), jnp.where(second, mine, other)])


def after(value, *earlier):
    return lax.optimization_barrier((value,) + earlier)[0]


def per_device(features):
    r = lax.axis_index("row")
    c = lax.axis_index("col")
    z, core = r // 2, r % 2
    x, y = c // 4, c % 4
    pos = jnp.concatenate([jnp.stack([r, c]), jnp.array(HOSTS).reshape(-1)]).astype(jnp.int32)
    own = lax.optimization_barrier(jnp.where(r >= 0, features[:, 0], 0))

    together = lambda *values: lax.optimization_barrier(values)

    first_a = own[0]
    first_b = swap_row(first_a, 0, 1)
    rows_b = swap_col(own, 0, 1)
    first = ordered(first_a, first_b, core == 1)

    got = swap_row(first, 1, 0)
    first, rows_b = together(jnp.where(z % 2 == 1, got, first), rows_b)

    got = swap_row(first, 3, 0)
    rows = ordered(own, rows_b, y % 2 == 1)
    pair = rows.reshape(2, 6, 2, 16, T)
    rows_b = swap_col(rows, 0, 3)
    first, rows_b = together(jnp.where(z >= 2, got, first), rows_b)

    first_b = swap_col(first, 0, 1)
    rows = ordered(rows, rows_b, y >= 2).reshape(4, 12, 16, T)
    rows_b = swap_col(rows, 1, 0)
    first = ordered(first, first_b, y % 2 == 1)

    first_b = swap_col(first, 0, 3)
    first = ordered(first, first_b, y >= 2).reshape(4, 2, 16, T)

    first_b = swap_col(first, 3, 0)
    first, rows_b = together(ordered(first, first_b, x >= 2), rows_b)

    first_b = swap_col(first, 1, 0)
    rows = ordered(rows, rows_b, x % 2 == 1)
    rows_b = swap_col(rows, 3, 0)
    pair = after(jnp.where(c % 2 == 1, pair[:, :, 1], pair[:, :, 0]), first)
    route = [(q * 16 + s, HOSTS[s % 2 * 8 + q][s // 2] * 16 + s % 2 * 8 + q) for q in range(8) for s in range(16)]
    cols = lax.ppermute(pair, ("row", "col"), route)

    small = [((B, B), F32)] * 3
    u0, *state = factor_call(factor_start, "factor_start", [((N, T), BF)] + small, pos, first, first_b)
    u0, cols = together(u0, cols)
    cols_b = swap_row(cols, 1, 0)
    x0, lx, d1 = factor_call(
        factor_middle, "factor_middle", [((T, 3 * T), BF), ((T, T), F32), ((T, T), F32)], u0, *state
    )
    d1, cols_b = together(d1, cols_b)
    cols = ordered(cols, cols_b, z % 2 == 1)
    cols_b = swap_row(cols, 3, 0)
    state = factor_call(factor_next, "factor_next", small, d1)
    *state, cols_b = together(*state, cols_b)
    cols = ordered(cols, cols_b, z >= 2).reshape(4, 2, 6, 16, T)
    cols_b = swap_row(cols, 0, 1)
    (x1,) = factor_call(factor_end, "factor_end", [((T, 6 * T), BF)], *state, lx)

    schur, panels = schur_call(pos, rows, rows_b, cols, cols_b, u0, x0, x1)
    return schur.reshape(12, 1, T, 6, 1, T), panels[:, None]


def solution(mesh):
    return jax.shard_map(
        per_device,
        mesh=mesh,
        in_specs=(P(None, "row", "col", None),),
        out_specs=(P(None, "row", None, None, "col", None), P(None, "row", None, None)),
        check_vma=False,
    )
```

```python
import functools

import jax
import jax.numpy as jnp
from jax import lax
from jax.experimental import pallas as pl
from jax.experimental.pallas import tpu as pltpu
from jax.sharding import PartitionSpec as P

T = 256
N = 2 * T
B = 128
G = 8
BF = jnp.bfloat16
F32 = jnp.float32
SCALE = 2.0 * 1.4426950408889634
epsilon = 1e-06


def dot_nt(a, b):
    return lax.dot_general(a, b, (((1,), (1,)), ((), ())), preferred_element_type=F32)


def split(x):
    hi = x.astype(BF)
    return hi, (x - hi.astype(F32)).astype(BF)


def kern(u, v):
    return jnp.exp2(SCALE * dot_nt(u, v) - SCALE)


def normal(raw):
    f = raw.astype(F32)
    return (f * lax.rsqrt(jnp.sum(f * f, axis=-1, keepdims=True) + epsilon)).astype(BF)


def dot3(a, b, dims):
    ah, al = split(a)
    bh, bl = split(b)
    d = lambda x, y: lax.dot_general(x, y, (dims, ((), ())), preferred_element_type=F32)
    return d(ah, bh) + d(al, bh) + d(ah, bl)


def factor_block(a):
    eye = (lax.broadcasted_iota(jnp.int32, (B, B), 0) == lax.broadcasted_iota(jnp.int32, (B, B), 1)).astype(F32)
    n_g = B // G
    groups_a = [a[G * g : G * g + G] for g in range(n_g)]
    groups_b = [eye[G * g : G * g + G] for g in range(n_g)]
    out = []
    for g in range(n_g):
        cols = [
            [jnp.broadcast_to(groups_a[i][:, G * g + k : G * g + k + 1], (G, B)) for i in range(g, n_g)]
            for k in range(G)
        ]
        rows_a = [groups_a[g][k : k + 1] for k in range(G)]
        rows_b = [groups_b[g][k : k + 1] for k in range(G)]
        facs = []
        for k in range(G):
            scale = lax.rsqrt(cols[k][0][k : k + 1])
            fac = [x * scale for x in cols[k]]
            facs.append(fac)
            rows_a[k] = rows_a[k] * scale
            rows_b[k] = rows_b[k] * scale
            for m in range(k + 1, G):
                piv = fac[0][m : m + 1]
                cols[m] = [x - f * piv for x, f in zip(cols[m], fac)]
                rows_a[m] = rows_a[m] - piv * rows_a[k]
                rows_b[m] = rows_b[m] - piv * rows_b[k]
        out.append(jnp.concatenate(rows_b, axis=0))
        for i in range(g + 1, n_g):
            ga, gb = groups_a[i], groups_b[i]
            for k in range(G):
                ga = ga - facs[k][i - g] * rows_a[k]
                gb = gb - facs[k][i - g] * rows_b[k]
            groups_a[i], groups_b[i] = ga, gb
    return jnp.concatenate(out, axis=0)


def thrice(x, left):
    hi, lo = split(x)
    return jnp.concatenate([hi, lo, hi] if left else [hi, hi, lo], axis=1)


def picked(flag, second, mine, other):
    return jnp.where(flag, mine, other) if second else jnp.where(flag, other, mine)


def eliminate(top, k):
    w = dot3(top, k[:B, B:], ((1,), (0,)))
    return w, k[B:, B:] - dot3(w, w, ((0,), (0,)))


def joined(top, w, bottom):
    corner = dot3(bottom, dot3(w, top, ((0,), (0,))), ((1,), (0,)))
    return jnp.concatenate(
        [jnp.concatenate([top, jnp.zeros((B, B), F32)], axis=1), jnp.concatenate([-corner, bottom], axis=1)], axis=0
    )


def identity():
    return (lax.broadcasted_iota(jnp.int32, (T, T), 0) == lax.broadcasted_iota(jnp.int32, (T, T), 1)).astype(F32)


def factor_start(pos, mine, other, u0, top, w, rest):
    x = pos[1] // 4
    inner = jnp.logical_or(x == 1, x == 2)
    for t in range(2):
        for c in range(16):
            x, y = c // 4, c % 4
            block = picked(inner, int(x in (1, 2)), mine[x // 2, y, t], other[x // 2, y, t])
            u0[t * T + c * 16 : t * T + c * 16 + 16, :] = normal(block)
    u = u0[:T, :]
    k = kern(u, u) + identity()
    top[...] = factor_block(k[:B, :B])
    w[...], rest[...] = eliminate(top[...], k)


def factor_middle(u0, top, w, rest, x0, x, low, d1):
    u = u0[...]
    k10 = kern(u[T:], u[:T])
    k11 = kern(u[T:], u[T:]) + identity()
    x[...] = joined(top[...], w[...], factor_block(rest[...]))
    x0[...] = thrice(x[...], False)
    low[...] = dot_nt(thrice(k10, True), x0[...])
    d1[...] = k11 - dot_nt(thrice(low[...], True), thrice(low[...], False))


def factor_next(d1, x, low, top, w, rest, lx):
    d = d1[...]
    lx[...] = dot3(low[...], x[...], ((1,), (0,)))
    top[...] = factor_block(d[:B, :B])
    w[...], rest[...] = eliminate(top[...], d)


def factor_end(top, w, rest, lx, x1):
    x = joined(top[...], w[...], factor_block(rest[...]))
    x1[...] = thrice(jnp.concatenate([-dot3(x, lx[...], ((1,), (0,))), x], axis=1), False)


def factor_call(kernel, name, outs, *args):
    vmem = pl.BlockSpec(memory_space=pltpu.VMEM)
    place = lambda a: pl.BlockSpec(memory_space=pltpu.SMEM) if a.dtype == jnp.int32 else vmem
    return pl.pallas_call(
        kernel,
        out_shape=[jax.ShapeDtypeStruct(*o) for o in outs],
        in_specs=[place(a) for a in args],
        out_specs=[vmem] * len(outs),
        compiler_params=pltpu.CompilerParams(vmem_limit_bytes=16 * 2**20),
        cost_estimate=pl.CostEstimate(flops=4 * 10**9, bytes_accessed=10**6, transcendentals=T * N),
        name=name,
    )(*args)


def panel_rows(k, xs):
    kh, kl = split(k)
    out = []
    for b in range(2):
        n = (b + 1) * T
        out.append(dot_nt(jnp.concatenate([kh[:, :n], kl[:, :n], kh[:, :n]], axis=1), xs[b][...]))
    return out


def schur_kernel(pos, row_mine, row_other, col_mine, col_other, u0, x0, x1, schur, pan, pc, uc, *, tiles):
    step = pl.program_id(0)
    r, c = pos[0], pos[1]
    height = tiles * T

    @pl.when(step == 0)
    def _():
        for j in range(6):
            for s in range(16):
                host = pos[2 + c * 8 + s // 2]
                z, e = host // 2, s % 2
                block = jnp.where(host % 2 == r % 2, col_mine[z, e, j], col_other[z, e, j])
                uc[j, s * 16 : s * 16 + 16, :] = normal(block)
            k = kern(uc[j], u0[...])
            if j == 0:
                rows = lax.broadcasted_iota(jnp.int32, (T, N), 0) + c * T
                k = k + (rows == lax.broadcasted_iota(jnp.int32, (T, N), 1)).astype(F32)
            (h0, l0), (h1, l1) = [split(p) for p in panel_rows(k, (x0, x1))]
            pc[j] = jnp.concatenate([h0, h1, h0, h1, l0, l1], axis=1)

    x_hi = c // 4 >= 2
    blocks = []
    for t in range(tiles):
        for s in range(16):
            x, y = s // 4, s % 4
            low, high = row_mine[x % 2, y, t], row_other[x % 2, y, t]
            blocks.append(picked(x_hi, x // 2, low, high))
    u = normal(jnp.concatenate(blocks, axis=0))
    k = kern(u, u0[...])
    rows = lax.broadcasted_iota(jnp.int32, (height, N), 0)
    cols = lax.broadcasted_iota(jnp.int32, (height, N), 1)
    shift = jnp.where(jnp.logical_and(step == 0, r < 2), r * T, N)
    rows = rows + jnp.where(rows < T, shift, N)
    k = k + (rows == cols).astype(F32)
    p = jnp.concatenate(panel_rows(k, (x0, x1)), axis=1)
    p = jnp.where(rows >= cols, p, 0.0)
    for t in range(tiles):
        pan[t] = p[t * T : (t + 1) * T]
    hi, lo = split(p)
    left = jnp.concatenate([hi, lo, hi], axis=1)
    for j in range(6):
        s = kern(u, uc[j]) - dot_nt(left, pc[j])
        for t in range(tiles):
            for h in range(2):
                schur[pl.ds(t * T * 12 + j * 2 + h, T, stride=12), :] = s[t * T : (t + 1) * T, h * 128 : h * 128 + 128]
    for t in range(tiles):
        a = step * tiles + t

        @pl.when(jnp.logical_and(r == c % 8, (a - c // 8) % 2 == 0))
        def _():
            j = (a - c // 8) // 2
            for h in range(2):
                where = pl.ds(t * T * 12 + j * 2 + h, T, stride=12)
                i = lax.broadcasted_iota(jnp.int32, (T, 128), 0)
                l = lax.broadcasted_iota(jnp.int32, (T, 128), 1) + h * 128
                schur[where, :] = schur[where, :] + (i == l).astype(F32)


def schur_call(pos, row_mine, row_other, col_mine, col_other, u0, x0, x1, tiles=3):
    full = lambda a: pl.BlockSpec(a.shape, lambda i, _: (0,) * a.ndim)
    rows = pl.BlockSpec((2, 4, tiles, 16, T), lambda i, _: (0, 0, i, 0, 0))
    return pl.pallas_call(
        functools.partial(schur_kernel, tiles=tiles),
        grid_spec=pltpu.PrefetchScalarGridSpec(
            num_scalar_prefetch=1,
            grid=(12 // tiles,),
            in_specs=[rows, rows] + [full(a) for a in (col_mine, col_other, u0, x0, x1)],
            out_specs=[
                pl.BlockSpec((tiles * T * 12, 128), lambda i, _: (i, 0)),
                pl.BlockSpec((tiles, T, N), lambda i, _: (i, 0, 0)),
            ],
            scratch_shapes=[pltpu.VMEM((6, T, 6 * T), BF), pltpu.VMEM((6, T, T), BF)],
        ),
        out_shape=[
            jax.ShapeDtypeStruct((12 * T * 12, 128), F32),
            jax.ShapeDtypeStruct((12, T, N), F32),
        ],
        compiler_params=pltpu.CompilerParams(vmem_limit_bytes=40 * 2**20, dimension_semantics=("arbitrary",)),
        cost_estimate=pl.CostEstimate(flops=24 * 10**9, bytes_accessed=30 * 10**6, transcendentals=7 * 10**6),
        name="schur",
    )(pos, row_mine, row_other, col_mine, col_other, u0, x0, x1)


def hops(a, b):
    return min((a - b) % 4, (b - a) % 4)


def host_rows(column):
    row, odd = column % 8, column // 8
    far = lambda p: hops(p // 2, column // 4) + hops(p % 2 * 2 + odd, column % 4)
    pairs = sorted(range(8), key=lambda p: (-far(p), p))
    rows = sorted(range(8), key=lambda r: (hops(r // 2, row // 2), r))
    return [rows[pairs.index(p)] for p in range(8)]


HOSTS = [host_rows(column) for column in range(16)]


def swap_row(value, flip_z, flip_core):
    pairs = [(r, (((r >> 1) ^ flip_z) << 1) | ((r & 1) ^ flip_core)) for r in range(8)]
    return lax.ppermute(value, "row", pairs)


def swap_col(value, flip_x, flip_y):
    pairs = [(c, (((c >> 2) ^ flip_x) << 2) | ((c & 3) ^ flip_y)) for c in range(16)]
    return lax.ppermute(value, "col", pairs)


def ordered(mine, other, second):
    return jnp.stack([jnp.where(second, other, mine), jnp.where(second, mine, other)])


def after(value, *earlier):
    return lax.optimization_barrier((value,) + earlier)[0]


def per_device(features):
    r = lax.axis_index("row")
    c = lax.axis_index("col")
    z, core = r // 2, r % 2
    x, y = c // 4, c % 4
    pos = jnp.concatenate([jnp.stack([r, c]), jnp.array(HOSTS).reshape(-1)]).astype(jnp.int32)
    own = lax.optimization_barrier(jnp.where(r >= 0, features[:, 0], 0))

    together = lambda *values: lax.optimization_barrier(values)

    first_a = own[0]
    first_b = swap_row(first_a, 0, 1)
    rows_b = swap_col(own, 0, 1)
    first = ordered(first_a, first_b, core == 1)

    got = swap_row(first, 1, 0)
    first, rows_b = together(jnp.where(z % 2 == 1, got, first), rows_b)

    got = swap_row(first, 3, 0)
    rows = ordered(own, rows_b, y % 2 == 1)
    pair = rows.reshape(2, 6, 2, 16, T)
    rows_b = swap_col(rows, 0, 3)
    first, rows_b = together(jnp.where(z >= 2, got, first), rows_b)

    first_b = swap_col(first, 0, 1)
    rows = ordered(rows, rows_b, y >= 2).reshape(4, 12, 16, T)
    rows_b = swap_col(rows, 1, 0)
    first = ordered(first, first_b, y % 2 == 1)

    first_b = swap_col(first, 0, 3)
    first = ordered(first, first_b, y >= 2).reshape(4, 2, 16, T)

    pair = after(jnp.where(c % 2 == 1, pair[:, :, 1], pair[:, :, 0]), first)
    route = [(q * 16 + s, HOSTS[s % 2 * 8 + q][s // 2] * 16 + s % 2 * 8 + q) for q in range(8) for s in range(16)]
    cols = lax.ppermute(pair, ("row", "col"), route)

    first_b = swap_col(first, 3, 0)
    first, rows_b = together(ordered(first, first_b, x >= 2), rows_b)

    first_b = swap_col(first, 1, 0)
    rows = ordered(rows, rows_b, x % 2 == 1)
    rows_b = swap_col(rows, 3, 0)
    small = [((B, B), F32)] * 3
    u0, *state = factor_call(factor_start, "factor_start", [((N, T), BF)] + small, pos, first, first_b)
    u0, cols = together(u0, cols)
    cols_b = swap_row(cols, 1, 0)
    tile = ((T, T), F32)
    x0, x_top, low, d1 = factor_call(
        factor_middle, "factor_middle", [((T, 3 * T), BF), tile, tile, tile], u0, *state
    )
    d1, cols_b = together(d1, cols_b)
    cols = ordered(cols, cols_b, z % 2 == 1)
    cols_b = swap_row(cols, 3, 0)
    *state, lx = factor_call(factor_next, "factor_next", small + [tile], d1, x_top, low)
    *state, cols_b = together(*state, cols_b)
    cols = ordered(cols, cols_b, z >= 2).reshape(4, 2, 6, 16, T)
    cols_b = swap_row(cols, 0, 1)
    (x1,) = factor_call(factor_end, "factor_end", [((T, 6 * T), BF)], *state, lx)

    schur, panels = schur_call(pos, rows, rows_b, cols, cols_b, u0, x0, x1)
    return schur.reshape(12, 1, T, 6, 1, T), panels[:, None]


def solution(mesh):
    return jax.shard_map(
        per_device,
        mesh=mesh,
        in_specs=(P(None, "row", "col", None),),
        out_specs=(P(None, "row", None, None, "col", None), P(None, "row", None, None)),
        check_vma=False,
    )
```
